32 devices in a mesh: rows: 16 (over z, x, core), chan: 2 (over y).
Axes of the slice: x: 2, y: 2, z: 4, core: 2. Of those that a mesh axis runs over, the one named last changes fastest.
Arguments:
- feature: bfloat16 [48, 144, 1536], P('rows', None, 'chan'), may hold values from -6 to 6
- kernel: float32 [7, 7, 1536], P(None, None, 'chan'), may hold values from -0.875 to 0.875
- ln_gain: float32 [1536], replicated, may hold values from 0.1 to 1.9
- layer_scale: float32 [1536], replicated, may hold values from 0.1 to 1.9
- w_in: bfloat16 [1536, 6144], P(None, 'chan'), may hold values from -0.15625 to 0.15625
- w_out: bfloat16 [6144, 1536], P('chan'), may hold values from -0.078125 to 0.078125
- cotangent: bfloat16 [48, 144, 1536], P('rows'), may hold values from -6 to 6
Outputs:
- grad_feature: bfloat16 [48, 144, 1536], P('rows', None, 'chan')
- grad_w_in: float32 [1536, 6144], P('rows', 'chan')
- grad_w_out: float32 [6144, 1536], P('chan', 'rows')
- grad_kernel: float32 [7, 7, 1536], P(None, None, 'chan')
The draws below stay inside these ranges and needn't reach their ends.
All inputs are finite; a program needn't handle non-finite values.
Results may differ from the reference program's by a relative error of at most 0.03.
Values may be sent and summed in bfloat16 or wider, within the bound.
A program may use at most 128 MiB of HBM per device.

```python
import math
import jax
import jax.numpy as jnp
from jax import lax

C = 1536
FF = 6144
KS = 7
ROWS_DEV = 3
COLS = 144
ROWS_ALL = 48
N_ROWS = 16


def spiked(entries, rng, source, target, blocks, factor):
    owner, partner = [(jnp.arange(entries.shape[position]) // (entries.shape[position] // blocks)).reshape([-1 if axis == position else 1 for axis in range(entries.ndim)]) for position in (source, target)]
    chosen = jax.random.permutation(rng, blocks)[partner]
    strong = (owner == chosen) | (owner == (partner + blocks // 2) % blocks)
    return jnp.where(strong, factor * entries, entries)


def block_scale(rng, shape, cuts, smallest, high):
    def one(position, shards_of):
        draws = jax.random.uniform(jax.random.fold_in(jax.random.fold_in(rng, 6), position), (shards_of,), jnp.float32, smallest / len(cuts), high / len(cuts))
        return jnp.repeat(jnp.exp(draws), shape[position] // shards_of).reshape((-1,) + (1,) * (len(shape) - position - 1))

    gain = one(*cuts[0])
    for cut in cuts[1:]:
        gain = gain * one(*cut)
    return gain


def bell_draw(own_key, dims, scale, limit, pieces=(), dtype=jnp.bfloat16):
    values = scale * jax.random.normal(own_key, dims, jnp.float32)
    if pieces:
        values = values * block_scale(own_key, dims, pieces, -0.22, 0.18)
    return jnp.clip(values, -limit, limit).astype(dtype)


def bell_draw_with(rng, extent, deviation, limit, pieces, heavy, dtype=jnp.bfloat16):
    values = deviation * jax.random.normal(rng, extent, jnp.float32)
    if pieces:
        values = values * block_scale(rng, extent, pieces, -0.22, 0.18)
    return jnp.clip(spiked(values, jax.random.fold_in(rng, 3), *heavy), -limit, limit).astype(dtype)


def setup_inputs(seed: int = 0) -> dict:
    streams_of = jax.random.split(jax.random.key(seed), 8)
    return {
        "feature": bell_draw(streams_of[0], (ROWS_ALL, COLS, C), 1.0, 6.0, ((0, 16), (2, 2))),
        "kernel": bell_draw(streams_of[1], (KS, KS, C), (KS * KS) ** -0.5, 0.875, ((2, 2),), jnp.float32),
        "ln_gain": jnp.clip(1.0 + 0.18 * jax.random.normal(streams_of[2], (C,), jnp.float32), 0.1, 1.9),
        "layer_scale": jnp.clip(1.0 + 0.18 * jax.random.normal(streams_of[3], (C,), jnp.float32), 0.1, 1.9),
        "w_in": bell_draw(streams_of[4], (C, FF), C ** -0.5, 0.15625, ((1, 2),)),
        "w_out": bell_draw(streams_of[5], (FF, C), FF ** -0.5, 0.078125, ((0, 2),)),
        "cotangent": bell_draw_with(streams_of[6], (ROWS_ALL, COLS, C), 1.0, 6.0, ((0, 16),), (0, 2, 16, 2.0)),
    }


def conv_taps(padded, kernel, height, width):
    result = jnp.zeros((height, width, kernel.shape[2]), jnp.float32)
    for tap_row in range(KS):
        for tap_col in range(KS):
            window = padded[tap_row:tap_row + height, tap_col:tap_col + width].astype(jnp.float32)
            result = result + window * kernel[tap_row, tap_col]
    return result

def conv_back(grad_pad, kernel, height, width):
    result = jnp.zeros((height, width, kernel.shape[2]), jnp.float32)
    for tap_row in range(KS):
        for tap_col in range(KS):
            window = grad_pad[6 - tap_row:6 - tap_row + height, 6 - tap_col:6 - tap_col + width].astype(jnp.float32)
            result = result + window * kernel[tap_row, tap_col]
    return result

def kernel_terms(grad_conv, padded, height, width):
    grad_float = grad_conv.astype(jnp.float32)
    rows_list = []
    for tap_row in range(KS):
        cols_list = []
        for tap_col in range(KS):
            window = padded[tap_row:tap_row + height, tap_col:tap_col + width].astype(jnp.float32)
            cols_list.append(lax.optimization_barrier(jnp.sum(grad_float * window, axis=(0, 1))))
        rows_list.append(jnp.stack(cols_list))
    return jnp.stack(rows_list)

def gelu_tanh(value):
    return jax.nn.gelu(value, approximate=True)

def reference(feature, kernel, ln_gain, layer_scale, w_in, w_out, cotangent):
    scale = 1.0 / math.sqrt(ROWS_ALL * COLS)
    padded = jnp.pad(feature, ((3, 3), (3, 3), (0, 0)))
    conv_out = conv_taps(padded, kernel, ROWS_ALL, COLS).astype(jnp.bfloat16)
    pixels = ROWS_DEV * COLS
    conv_blocks = conv_out.reshape(N_ROWS, pixels, C)
    cot_blocks = cotangent.reshape(N_ROWS, pixels, C)

    def block_step(carry, pair):
        conv_blk, cot_blk = pair
        values = conv_blk.astype(jnp.float32)
        mean = lax.optimization_barrier(jnp.mean(values, axis=1, keepdims=True))
        centred = values - mean
        var = lax.optimization_barrier(jnp.mean(centred * centred, axis=1, keepdims=True))
        rstd = 1.0 / jnp.sqrt(var + 1e-06)
        nhat = centred * rstd
        normed = (nhat * ln_gain).astype(jnp.bfloat16)
        hidden = jnp.dot(normed, w_in, preferred_element_type=jnp.float32)
        activ = gelu_tanh(hidden).astype(jnp.bfloat16)
        grad_mixed = (cot_blk.astype(jnp.float32) * layer_scale).astype(jnp.bfloat16)
        grad_activ = lax.dot_general(grad_mixed, w_out, (((1,), (1,)), ((), ())), preferred_element_type=jnp.float32)
        grad_hidden = jax.vjp(gelu_tanh, hidden)[1](grad_activ)[0].astype(jnp.bfloat16)
        part_out = lax.dot_general(activ, grad_mixed, (((0,), (0,)), ((), ())), preferred_element_type=jnp.float32)
        part_in = lax.dot_general(normed, grad_hidden, (((0,), (0,)), ((), ())), preferred_element_type=jnp.float32)
        grad_normed = lax.dot_general(grad_hidden, w_in, (((1,), (1,)), ((), ())), preferred_element_type=jnp.float32)
        scaled = grad_normed * ln_gain
        first_mean = lax.optimization_barrier(jnp.mean(scaled, axis=1, keepdims=True))
        second_mean = lax.optimization_barrier(jnp.mean(scaled * nhat, axis=1, keepdims=True))
        grad_conv = (rstd * (scaled - first_mean - nhat * second_mean)).astype(jnp.bfloat16)
        return ((carry[0] + part_in, carry[1] + part_out), grad_conv)
    start = (jnp.zeros((C, FF), jnp.float32), jnp.zeros((FF, C), jnp.float32))
    totals, grad_blocks = lax.scan(block_step, start, (conv_blocks, cot_blocks))
    grad_conv = grad_blocks.reshape(ROWS_ALL, COLS, C)
    grad_pad = jnp.pad(grad_conv, ((3, 3), (3, 3), (0, 0)))
    grad_feature = (cotangent.astype(jnp.float32) + conv_back(grad_pad, kernel, ROWS_ALL, COLS)).astype(jnp.bfloat16)
    grad_kernel = kernel_terms(grad_conv, padded, ROWS_ALL, COLS) * scale
    return (grad_feature, totals[0] * scale, totals[1] * scale, grad_kernel)
```

```python
import math

import jax
import jax.numpy as jnp
from jax import lax
from jax.sharding import PartitionSpec as P


def halo(cells, width):
    count = lax.axis_size("rows")
    ends = count - 1
    head = cells[:width]
    tail = cells[cells.shape[0] - width :]
    above = lax.ppermute(tail, "rows", [(i, i + 1) for i in range(ends)])
    below = lax.ppermute(head, "rows", [(i + 1, i) for i in range(ends)])
    return jnp.concatenate([above, cells, below], axis=0)


def conv_taps(padded, kernel, height, width):
    result = jnp.zeros((height, width, kernel.shape[2]), jnp.float32)
    for tap_row in range(7):
        for tap_col in range(7):
            window = padded[tap_row : tap_row + height, tap_col : tap_col + width].astype(
                jnp.float32
            )
            result = result + window * kernel[tap_row, tap_col]
    return result


def conv_back(grad_pad, kernel, height, width):
    result = jnp.zeros((height, width, kernel.shape[2]), jnp.float32)
    for tap_row in range(7):
        for tap_col in range(7):
            window = grad_pad[
                6 - tap_row : 6 - tap_row + height, 6 - tap_col : 6 - tap_col + width
            ].astype(jnp.float32)
            result = result + window * kernel[tap_row, tap_col]
    return result


def kernel_terms(grad_conv, padded, height, width):
    grad_float = grad_conv.astype(jnp.float32)
    rows_list = []
    for tap_row in range(7):
        cols_list = []
        for tap_col in range(7):
            window = padded[tap_row : tap_row + height, tap_col : tap_col + width].astype(
                jnp.float32
            )
            cols_list.append(jnp.sum(grad_float * window, axis=(0, 1)))
        rows_list.append(jnp.stack(cols_list))
    return jnp.stack(rows_list)


def gelu_tanh(value):
    return jax.nn.gelu(value, approximate=True)


def chip_at(place, chips):
    place = place % chips
    half = chips // 2
    return jnp.where(place < half, 2 * place, 2 * (chips - 1 - place) + 1)


def ring_pairs(chips, step):
    def chip(place):
        place = place % chips
        half = chips // 2
        return 2 * place if place < half else 2 * (chips - 1 - place) + 1

    return [
        (2 * chip(p) + core, 2 * chip(p + step) + core) for p in range(chips) for core in range(2)
    ]


def ring_sums(part, place, chips):
    share = part.shape[0] // chips
    half = share // 2

    def piece(position, side):
        return lax.dynamic_slice_in_dim(
            part, chip_at(position, chips) * share + side * half, half, 0
        )

    sums = [piece(place + chips - 1, 0), piece(place + 1, 1)]
    for step in range(chips - 1):
        for side, way in ((0, 1), (1, -1)):
            got = lax.ppermute(sums[side], "rows", ring_pairs(chips, way))
            own = piece(place + 2 * chips - way * (2 + step), side)
            total = got.astype(jnp.float32) + own.astype(jnp.float32)
            sums[side] = total.astype(jnp.bfloat16)
    return sums


def own_rows(sums, core, swap):
    mine = jnp.where(core == 0, sums[0], sums[1])
    theirs = jnp.where(core == 0, sums[1], sums[0])
    got = lax.ppermute(theirs, "rows", swap)
    first = jnp.where(core == 0, mine, got)
    second = jnp.where(core == 0, got, mine)
    return jnp.concatenate([first, second], axis=1).astype(jnp.float32)


def shards(feature, kernel, ln_gain, layer_scale, w_in, w_out, cotangent):
    height, width, local_ch = feature.shape
    channels = cotangent.shape[2]
    pixels = height * width
    rows = lax.axis_size("rows")
    chan = lax.axis_size("chan")
    chips = rows // 2
    me = lax.axis_index("rows")
    lane = lax.axis_index("chan")
    core = me % 2
    chip = me // 2
    place = jnp.where(chip % 2 == 0, chip // 2, chips - 1 - chip // 2)
    swap = [(i, i ^ 1) for i in range(rows)]
    cross = [(0, 1), (1, 0)]
    scale = 1.0 / math.sqrt(height * rows * width)
    offset = lane * local_ch
    units = w_in.shape[1] // 2

    rimmed = halo(feature, 3)
    grad_mixed = (cotangent.reshape(pixels, channels).astype(jnp.float32) * layer_scale).astype(
        jnp.bfloat16
    )
    mixed_both = jnp.concatenate([grad_mixed, lax.ppermute(grad_mixed, "rows", swap)], axis=0)
    in_part = lax.dynamic_slice_in_dim(w_in, core * units, units, 1)
    out_part = lax.dynamic_slice_in_dim(w_out, core * units, units, 0)

    padded = jnp.pad(rimmed, ((0, 0), (3, 3), (0, 0)))
    conv_local = conv_taps(padded, kernel, height, width).astype(jnp.bfloat16)
    conv_local = conv_local.reshape(pixels, local_ch)
    if chan == 2:
        conv_other = lax.ppermute(conv_local, "chan", cross)
        conv_full = jnp.concatenate(
            [
                jnp.where(lane == 0, conv_local, conv_other),
                jnp.where(lane == 0, conv_other, conv_local),
            ],
            axis=1,
        )
    else:
        conv_full = lax.all_gather(conv_local, "chan", axis=1, tiled=True)
    grad_activ = lax.dot_general(
        mixed_both, out_part, (((1,), (1,)), ((), ())), preferred_element_type=jnp.float32
    )
    values = conv_full.astype(jnp.float32)
    mean = jnp.mean(values, axis=1, keepdims=True)
    centred = values - mean
    var = jnp.mean(centred * centred, axis=1, keepdims=True)
    rstd = 1.0 / jnp.sqrt(var + 1e-06)
    nhat = centred * rstd
    normed = (nhat * ln_gain).astype(jnp.bfloat16)
    normed_both = jnp.concatenate([normed, lax.ppermute(normed, "rows", swap)], axis=0)
    hidden = jnp.dot(normed_both, in_part, preferred_element_type=jnp.float32)
    activ = gelu_tanh(hidden).astype(jnp.bfloat16)
    grad_hidden = jax.vjp(gelu_tanh, hidden)[1](grad_activ)[0].astype(jnp.bfloat16)

    def pixel_sum(left, right):
        total = lax.dot_general(
            left, right, (((0,), (0,)), ((), ())), preferred_element_type=jnp.float32
        )
        return (total * scale).astype(jnp.bfloat16)

    def back(grads):
        return lax.dot_general(
            grads, in_part, (((1,), (1,)), ((), ())), preferred_element_type=jnp.float32
        )

    out_sums = ring_sums(pixel_sum(mixed_both, activ), place, chips)
    back_other = lax.ppermute(back(grad_hidden[pixels:]).astype(jnp.bfloat16), "rows", swap)
    back_own = back(grad_hidden[:pixels]) + back_other.astype(jnp.float32)
    in_sums = ring_sums(pixel_sum(normed_both, grad_hidden), place, chips)

    scaled_part = back_own * ln_gain
    first_part = jnp.sum(scaled_part, axis=1)
    second_part = jnp.sum(scaled_part * nhat, axis=1)
    pair = jnp.stack([first_part, second_part])
    if chan == 2:
        kept = lax.dynamic_slice_in_dim(back_own, offset, local_ch, 1)
        given = lax.dynamic_slice_in_dim(back_own, local_ch - offset, local_ch, 1)
        got = lax.ppermute(given.astype(jnp.bfloat16), "chan", cross).astype(jnp.float32)
        grad_normed = kept + got
        pair = pair + lax.ppermute(pair, "chan", cross)
    else:
        grad_normed = lax.psum_scatter(
            back_own.astype(jnp.bfloat16), "chan", scatter_dimension=1, tiled=True
        ).astype(jnp.float32)
        pair = lax.psum(pair, "chan")
    first_mean = pair[0][:, None] / channels
    second_mean = pair[1][:, None] / channels
    nhat_own = (conv_local.astype(jnp.float32) - mean) * rstd
    scaled = grad_normed * lax.dynamic_slice_in_dim(ln_gain, offset, local_ch, 0)
    grad_local = rstd * (scaled - first_mean - nhat_own * second_mean)
    grad_conv = grad_local.astype(jnp.bfloat16).reshape(height, width, local_ch)
    grad_rimmed = halo(grad_conv, 3)
    kernel_sum = (kernel_terms(grad_conv, padded, height, width) * scale).astype(jnp.bfloat16)
    grad_pad = jnp.pad(grad_rimmed, ((0, 0), (3, 3), (0, 0)))
    cot_own = lax.dynamic_slice_in_dim(cotangent, offset, local_ch, 2).astype(jnp.float32)
    grad_feature = (cot_own + conv_back(grad_pad, kernel, height, width)).astype(jnp.bfloat16)
    span = 1
    while span < rows:
        other = lax.ppermute(kernel_sum, "rows", [(i, i ^ span) for i in range(rows)])
        total = kernel_sum.astype(jnp.float32) + other.astype(jnp.float32)
        span *= 2
        kernel_sum = total if span >= rows else total.astype(jnp.bfloat16)
    grad_w_out = own_rows(out_sums, core, swap).T
    grad_w_in = own_rows(in_sums, core, swap)
    return (grad_feature, grad_w_in, grad_w_out, kernel_sum)


def solution(mesh):
    placed = (
        P("rows", None, "chan"),
        P(None, None, "chan"),
        P(),
        P(),
        P(None, "chan"),
        P("chan", None),
        P("rows", None, None),
    )
    return jax.shard_map(
        shards,
        mesh=mesh,
        in_specs=placed,
        out_specs=(
            P("rows", None, "chan"),
            P("rows", "chan"),
            P("chan", "rows"),
            P(None, None, "chan"),
        ),
        check_vma=False,
    )
```

```python
import math

import jax
import jax.numpy as jnp
from jax import lax
from jax.sharding import PartitionSpec as P


def halo(cells, width):
    count = lax.axis_size("rows")
    ends = count - 1
    head = cells[:width]
    tail = cells[cells.shape[0] - width :]
    above = lax.ppermute(tail, "rows", [(i, i + 1) for i in range(ends)])
    below = lax.ppermute(head, "rows", [(i + 1, i) for i in range(ends)])
    return above, below


def conv_taps(padded, kernel, height, width):
    result = jnp.zeros((height, width, kernel.shape[2]), jnp.float32)
    for tap_row in range(7):
        for tap_col in range(7):
            window = padded[tap_row : tap_row + height, tap_col : tap_col + width].astype(
                jnp.float32
            )
            result = result + window * kernel[tap_row, tap_col]
    return result


def conv_back(grad_pad, kernel, height, width):
    result = jnp.zeros((height, width, kernel.shape[2]), jnp.float32)
    for tap_row in range(7):
        for tap_col in range(7):
            window = grad_pad[
                6 - tap_row : 6 - tap_row + height, 6 - tap_col : 6 - tap_col + width
            ].astype(jnp.float32)
            result = result + window * kernel[tap_row, tap_col]
    return result


def kernel_terms(grad_conv, padded, height, width, tap_rows):
    grad_float = grad_conv.astype(jnp.float32)
    rows_list = []
    for tap_row in tap_rows:
        cols_list = []
        for tap_col in range(7):
            window = padded[tap_row : tap_row + height, tap_col : tap_col + width].astype(
                jnp.float32
            )
            cols_list.append(jnp.sum(grad_float * window, axis=(0, 1)))
        rows_list.append(jnp.stack(cols_list))
    return jnp.stack(rows_list)


def gelu_tanh(value):
    return jax.nn.gelu(value, approximate=True)


def chip_at(place, chips):
    place = lax.rem(place, chips)
    half = chips // 2
    return jnp.where(place < half, 2 * place, 2 * (chips - 1 - place) + 1)


def ring_pairs(chips, step):
    def chip(place):
        place = place % chips
        half = chips // 2
        return 2 * place if place < half else 2 * (chips - 1 - place) + 1

    return [
        (2 * chip(p) + core, 2 * chip(p + step) + core) for p in range(chips) for core in range(2)
    ]


def tie(value, *first):
    return lax.optimization_barrier((value, first))[0]


def ring_piece(part, position, side, chips):
    share = part.shape[0] // chips
    half = share // 2
    return lax.dynamic_slice_in_dim(
        part, chip_at(position, chips) * share + side * half, half, 0
    )


def ring_first(part, place, chips):
    return [ring_piece(part, place + chips - 1, 0, chips), ring_piece(part, place + 1, 1, chips)]


def ring_step(part, sums, step, place, chips):
    result = []
    for side, way in ((0, 1), (1, -1)):
        got = lax.ppermute(sums[side], "rows", ring_pairs(chips, way))
        own = ring_piece(part, place + 2 * chips - way * (2 + step), side, chips)
        total = got.astype(jnp.float32) + own.astype(jnp.float32)
        result.append(total.astype(jnp.bfloat16))
    return result


def own_rows(sums, core, swap):
    mine = jnp.where(core == 0, sums[0], sums[1])
    theirs = jnp.where(core == 0, sums[1], sums[0])
    got = lax.ppermute(theirs, "rows", swap)
    first = jnp.where(core == 0, mine, got)
    second = jnp.where(core == 0, got, mine)
    return jnp.concatenate([first, second], axis=1).astype(jnp.float32)


def shards(feature, kernel, ln_gain, layer_scale, w_in, w_out, cotangent):
    height, width, local_ch = feature.shape
    channels = cotangent.shape[2]
    pixels = height * width
    rows = lax.axis_size("rows")
    chan = lax.axis_size("chan")
    chips = rows // 2
    me = lax.axis_index("rows")
    lane = lax.axis_index("chan")
    core = lax.rem(me, 2)
    chip = lax.div(me, 2)
    level = lax.div(chip, 2)
    place = jnp.where(lax.rem(chip, 2) == 0, level, chips - 1 - level)
    swap = [(i, i ^ 1) for i in range(rows)]
    cross = [(0, 1), (1, 0)]
    scale = 1.0 / math.sqrt(height * rows * width)
    offset = lane * local_ch
    units = w_in.shape[1] // 2

    above, below = halo(feature, 3)
    grad_mixed = (cotangent.reshape(pixels, channels).astype(jnp.float32) * layer_scale).astype(
        jnp.bfloat16
    )
    mixed_both = jnp.concatenate([grad_mixed, lax.ppermute(grad_mixed, "rows", swap)], axis=0)
    in_part = lax.dynamic_slice_in_dim(w_in, core * units, units, 1)
    out_part = lax.dynamic_slice_in_dim(w_out, core * units, units, 0)
    grad_activ = lax.dot_general(
        mixed_both, out_part, (((1,), (1,)), ((), ())), preferred_element_type=jnp.float32
    )
    above, below = tie((above, below), grad_activ, in_part)
    rimmed = jnp.concatenate([above, feature, below], axis=0)

    padded = jnp.pad(rimmed, ((0, 0), (3, 3), (0, 0)))
    lines = []
    passed = []
    for line in range(height):
        done = conv_taps(padded[line : line + 7], kernel, 1, width).astype(jnp.bfloat16)
        done = done.reshape(width, local_ch)
        if lines:
            done = tie(done, lines[-1])
        lines.append(done)
        if chan == 2:
            passed.append(lax.ppermute(done, "chan", cross))
    conv_local = jnp.concatenate(lines, axis=0)
    if chan == 2:
        conv_other = jnp.concatenate(passed, axis=0)
        conv_full = jnp.concatenate(
            [
                jnp.where(lane == 0, conv_local, conv_other),
                jnp.where(lane == 0, conv_other, conv_local),
            ],
            axis=1,
        )
    else:
        conv_full = lax.all_gather(conv_local, "chan", axis=1, tiled=True)
    values = conv_full.astype(jnp.float32)
    mean = jnp.mean(values, axis=1, keepdims=True)
    centred = values - mean
    var = jnp.mean(centred * centred, axis=1, keepdims=True)
    rstd = 1.0 / jnp.sqrt(var + 1e-06)
    nhat = centred * rstd
    normed = (nhat * ln_gain).astype(jnp.bfloat16)
    normed_both = jnp.concatenate([normed, lax.ppermute(normed, "rows", swap)], axis=0)
    hidden = jnp.dot(normed_both, in_part, preferred_element_type=jnp.float32)
    activ = gelu_tanh(hidden).astype(jnp.bfloat16)
    grad_hidden = jax.vjp(gelu_tanh, hidden)[1](grad_activ)[0].astype(jnp.bfloat16)

    def pixel_sum(left, right):
        total = lax.dot_general(
            left, right, (((0,), (0,)), ((), ())), preferred_element_type=jnp.float32
        )
        return (total * scale).astype(jnp.bfloat16)

    def back(grads):
        return lax.dot_general(
            grads, in_part, (((1,), (1,)), ((), ())), preferred_element_type=jnp.float32
        )

    out_total = pixel_sum(mixed_both, activ)
    back_other = lax.ppermute(back(grad_hidden[pixels:]).astype(jnp.bfloat16), "rows", swap)
    in_total = pixel_sum(normed_both, grad_hidden)
    back_own = back(tie(grad_hidden[:pixels], in_total)) + back_other.astype(jnp.float32)

    scaled_part = back_own * ln_gain
    first_part = jnp.sum(scaled_part, axis=1)
    second_part = jnp.sum(scaled_part * nhat, axis=1)
    pair = jnp.stack([first_part, second_part])
    if chan == 2:
        kept = lax.dynamic_slice_in_dim(back_own, offset, local_ch, 1)
        given = lax.dynamic_slice_in_dim(back_own, local_ch - offset, local_ch, 1)
        sent = (given.astype(jnp.bfloat16), pair)
        got = lax.ppermute(sent[0], "chan", cross).astype(jnp.float32)
        grad_normed = kept + got
        pair = pair + lax.ppermute(pair, "chan", cross)
    else:
        sent = (back_own, pair)
        grad_normed = lax.psum_scatter(
            back_own.astype(jnp.bfloat16), "chan", scatter_dimension=1, tiled=True
        ).astype(jnp.float32)
        pair = lax.psum(pair, "chan")
    first_mean = pair[0][:, None] / channels
    second_mean = pair[1][:, None] / channels
    nhat_own = (conv_local.astype(jnp.float32) - mean) * rstd
    scaled = grad_normed * lax.dynamic_slice_in_dim(ln_gain, offset, local_ch, 0)
    grad_local = rstd * (scaled - first_mean - nhat_own * second_mean)
    grad_conv = grad_local.astype(jnp.bfloat16).reshape(height, width, local_ch)
    grad_above, grad_below = halo(grad_conv, 3)
    grad_rimmed = jnp.concatenate([grad_above, grad_conv, grad_below], axis=0)
    grad_pad = jnp.pad(grad_rimmed, ((0, 0), (3, 3), (0, 0)))
    cot_own = lax.dynamic_slice_in_dim(cotangent, offset, local_ch, 2).astype(jnp.float32)

    def terms(grads, tap_rows):
        return (kernel_terms(grads, padded, height, width, tap_rows) * scale).astype(
            jnp.bfloat16
        )

    def feature_line(line, grads):
        back_line = conv_back(grads, kernel, 1, width)
        return (cot_own[line : line + 1] + back_line).astype(jnp.bfloat16)

    kernel_sum = None
    pieces = []
    feature_lines = []
    span = 1
    turns = 6 + max(height, rows.bit_length() - 1)

    def work(turn, last):
        nonlocal kernel_sum, span
        if turn == 0:
            return sent
        if turn == 1:
            return None
        if turn == 2:
            return grad_conv
        if turn in (3, 4, 5):
            taps = ((0, 1), (2, 3, 4), (5, 6))[turn - 3]
            pieces.append(terms(tie(grad_conv, last), taps))
            if turn == 5:
                kernel_sum = jnp.concatenate(pieces, axis=0)
            return pieces[-1]
        if turn - 6 < height:
            line = turn - 6
            feature_lines.append(feature_line(line, tie(grad_pad[line : line + 7], last)))
        if span < rows:
            other = lax.ppermute(kernel_sum, "rows", [(i, i ^ span) for i in range(rows)])
            total = kernel_sum.astype(jnp.float32) + other.astype(jnp.float32)
            span *= 2
            kernel_sum = total if span >= rows else total.astype(jnp.bfloat16)
        return (feature_lines[-1], kernel_sum)

    totals = [out_total, in_total]
    sums = [ring_first(total, place, chips) for total in totals]
    turn = 0
    for step in range(chips - 1):
        for which in range(2):
            if step > 0 and turn < turns:
                result = work(turn, sums[1 - which])
                if result is not None:
                    sums[which] = tie(sums[which], result)
                turn += 1
            sums[which] = ring_step(totals[which], sums[which], step, place, chips)
    while turn < turns:
        work(turn, sums)
        turn += 1
    grad_feature = jnp.concatenate(feature_lines, axis=0)
    grad_w_out = own_rows(sums[0], core, swap).T
    grad_w_in = own_rows(sums[1], core, swap)
    return (grad_feature, grad_w_in, grad_w_out, kernel_sum)


def solution(mesh):
    placed = (
        P("rows", None, "chan"),
        P(None, None, "chan"),
        P(),
        P(),
        P(None, "chan"),
        P("chan", None),
        P("rows", None, None),
    )
    return jax.shard_map(
        shards,
        mesh=mesh,
        in_specs=placed,
        out_specs=(
            P("rows", None, "chan"),
            P("rows", "chan"),
            P("chan", "rows"),
            P(None, None, "chan"),
        ),
        check_vma=False,
    )
```

```python
import math

import jax
import jax.numpy as jnp
from jax import lax
from jax.sharding import PartitionSpec as P


def halo(cells, width):
    count = lax.axis_size("rows")
    ends = count - 1
    head = cells[:width]
    tail = cells[cells.shape[0] - width :]
    above = lax.ppermute(tail, "rows", [(i, i + 1) for i in range(ends)])
    below = lax.ppermute(head, "rows", [(i + 1, i) for i in range(ends)])
    return above, below


def conv_taps(padded, kernel, height, width):
    result = jnp.zeros((height, width, kernel.shape[2]), jnp.float32)
    for tap_row in range(7):
        for tap_col in range(7):
            window = padded[tap_row : tap_row + height, tap_col : tap_col + width].astype(
                jnp.float32
            )
            result = result + window * kernel[tap_row, tap_col]
    return result


def conv_back(grad_pad, kernel, height, width):
    result = jnp.zeros((height, width, kernel.shape[2]), jnp.float32)
    for tap_row in range(7):
        for tap_col in range(7):
            window = grad_pad[
                6 - tap_row : 6 - tap_row + height, 6 - tap_col : 6 - tap_col + width
            ].astype(jnp.float32)
            result = result + window * kernel[tap_row, tap_col]
    return result


def kernel_terms(grad_conv, padded, height, width, tap_rows):
    grad_float = grad_conv.astype(jnp.float32)
    rows_list = []
    for tap_row in tap_rows:
        cols_list = []
        for tap_col in range(7):
            window = padded[tap_row : tap_row + height, tap_col : tap_col + width].astype(
                jnp.float32
            )
            cols_list.append(jnp.sum(grad_float * window, axis=(0, 1)))
        rows_list.append(jnp.stack(cols_list))
    return jnp.stack(rows_list)


def gelu_tanh(value):
    return jax.nn.gelu(value, approximate=True)


def tie(value, *first):
    return lax.optimization_barrier((value, first))[0]


def chip_sums(part, chips):
    groups = [[2 * chip + core for chip in range(chips)] for core in range(2)]
    return lax.psum_scatter(
        part, "rows", scatter_dimension=0, axis_index_groups=groups, tiled=True
    )


def own_rows(total, core, swap):
    half = total.shape[0] // 2
    sums = (total[:half], total[half:])
    mine = jnp.where(core == 0, sums[0], sums[1])
    theirs = jnp.where(core == 0, sums[1], sums[0])
    got = lax.ppermute(theirs, "rows", swap)
    first = jnp.where(core == 0, mine, got)
    second = jnp.where(core == 0, got, mine)
    return jnp.concatenate([first, second], axis=1).astype(jnp.float32)


def shards(feature, kernel, ln_gain, layer_scale, w_in, w_out, cotangent):
    height, width, local_ch = feature.shape
    channels = cotangent.shape[2]
    pixels = height * width
    rows = lax.axis_size("rows")
    chan = lax.axis_size("chan")
    chips = rows // 2
    me = lax.axis_index("rows")
    lane = lax.axis_index("chan")
    core = lax.rem(me, 2)
    swap = [(i, i ^ 1) for i in range(rows)]
    cross = [(0, 1), (1, 0)]
    scale = 1.0 / math.sqrt(height * rows * width)
    offset = lane * local_ch
    units = w_in.shape[1] // 2

    above, below = halo(feature, 3)
    grad_mixed = (cotangent.reshape(pixels, channels).astype(jnp.float32) * layer_scale).astype(
        jnp.bfloat16
    )
    mixed_both = jnp.concatenate([grad_mixed, lax.ppermute(grad_mixed, "rows", swap)], axis=0)
    in_part = lax.dynamic_slice_in_dim(w_in, core * units, units, 1)
    out_part = lax.dynamic_slice_in_dim(w_out, core * units, units, 0)
    grad_activ = lax.dot_general(
        mixed_both, out_part, (((1,), (1,)), ((), ())), preferred_element_type=jnp.float32
    )
    above, below = tie((above, below), mixed_both, out_part, in_part)
    rimmed = jnp.concatenate([above, feature, below], axis=0)

    padded = jnp.pad(rimmed, ((0, 0), (3, 3), (0, 0)))
    lines = []
    passed = []
    for line in range(height):
        done = conv_taps(padded[line : line + 7], kernel, 1, width).astype(jnp.bfloat16)
        done = done.reshape(width, local_ch)
        if lines:
            done = tie(done, lines[-1])
        lines.append(done)
        if chan == 2:
            passed.append(lax.ppermute(done, "chan", cross))
    conv_local = jnp.concatenate(lines, axis=0)
    if chan == 2:
        conv_other = jnp.concatenate(tie(passed, grad_activ), axis=0)
        conv_full = jnp.concatenate(
            [
                jnp.where(lane == 0, conv_local, conv_other),
                jnp.where(lane == 0, conv_other, conv_local),
            ],
            axis=1,
        )
    else:
        conv_full = lax.all_gather(conv_local, "chan", axis=1, tiled=True)
    values = conv_full.astype(jnp.float32)
    mean = jnp.mean(values, axis=1, keepdims=True)
    centred = values - mean
    var = jnp.mean(centred * centred, axis=1, keepdims=True)
    rstd = 1.0 / jnp.sqrt(var + 1e-06)
    nhat = centred * rstd
    normed = (nhat * ln_gain).astype(jnp.bfloat16)
    normed_both = jnp.concatenate([normed, lax.ppermute(normed, "rows", swap)], axis=0)
    hidden = jnp.dot(normed_both, in_part, preferred_element_type=jnp.float32)
    activ = gelu_tanh(hidden).astype(jnp.bfloat16)
    grad_hidden = jax.vjp(gelu_tanh, hidden)[1](grad_activ)[0].astype(jnp.bfloat16)

    def pixel_sum(left, right):
        total = lax.dot_general(
            left, right, (((0,), (0,)), ((), ())), preferred_element_type=jnp.float32
        )
        return (total * scale).astype(jnp.bfloat16)

    def back(grads):
        return lax.dot_general(
            grads, in_part, (((1,), (1,)), ((), ())), preferred_element_type=jnp.float32
        )

    out_sum = chip_sums(pixel_sum(mixed_both, activ), chips)
    back_other = lax.ppermute(back(grad_hidden[pixels:]).astype(jnp.bfloat16), "rows", swap)
    in_sum = chip_sums(pixel_sum(normed_both, grad_hidden), chips)
    back_own = back(grad_hidden[:pixels]) + back_other.astype(jnp.float32)

    scaled_part = back_own * ln_gain
    first_part = jnp.sum(scaled_part, axis=1)
    second_part = jnp.sum(scaled_part * nhat, axis=1)
    pair = jnp.stack([first_part, second_part])
    if chan == 2:
        kept = lax.dynamic_slice_in_dim(back_own, offset, local_ch, 1)
        given = lax.dynamic_slice_in_dim(back_own, local_ch - offset, local_ch, 1)
        got = lax.ppermute(given.astype(jnp.bfloat16), "chan", cross).astype(jnp.float32)
        grad_normed = kept + got
        pair = pair + lax.ppermute(pair, "chan", cross)
    else:
        grad_normed = lax.psum_scatter(
            back_own.astype(jnp.bfloat16), "chan", scatter_dimension=1, tiled=True
        ).astype(jnp.float32)
        pair = lax.psum(pair, "chan")
    first_mean = pair[0][:, None] / channels
    second_mean = pair[1][:, None] / channels
    nhat_own = (conv_local.astype(jnp.float32) - mean) * rstd
    scaled = grad_normed * lax.dynamic_slice_in_dim(ln_gain, offset, local_ch, 0)
    grad_local = rstd * (scaled - first_mean - nhat_own * second_mean)
    grad_conv = grad_local.astype(jnp.bfloat16).reshape(height, width, local_ch)
    grad_above, grad_below = halo(grad_conv, 3)
    grad_rimmed = jnp.concatenate([grad_above, grad_conv, grad_below], axis=0)
    grad_pad = jnp.pad(grad_rimmed, ((0, 0), (3, 3), (0, 0)))
    cot_own = lax.dynamic_slice_in_dim(cotangent, offset, local_ch, 2).astype(jnp.float32)

    def terms(grads, tap_rows):
        return (kernel_terms(grads, padded, height, width, tap_rows) * scale).astype(
            jnp.bfloat16
        )

    def feature_line(line, grads):
        back_line = conv_back(grads, kernel, 1, width)
        return (cot_own[line : line + 1] + back_line).astype(jnp.bfloat16)

    kernel_sum = terms(grad_conv, range(7))
    lines = [feature_line(line, grad_pad[line : line + 7]) for line in range(height)]
    grad_feature = jnp.concatenate(lines, axis=0)
    span = 1
    while span < rows:
        other = lax.ppermute(kernel_sum, "rows", [(i, i ^ span) for i in range(rows)])
        total = kernel_sum.astype(jnp.float32) + other.astype(jnp.float32)
        span *= 2
        kernel_sum = total if span >= rows else total.astype(jnp.bfloat16)
    grad_w_out = own_rows(out_sum, core, swap).T
    grad_w_in = own_rows(in_sum, core, swap)
    return (grad_feature, grad_w_in, grad_w_out, kernel_sum)


def solution(mesh):
    placed = (
        P("rows", None, "chan"),
        P(None, None, "chan"),
        P(),
        P(),
        P(None, "chan"),
        P("chan", None),
        P("rows", None, None),
    )
    return jax.shard_map(
        shards,
        mesh=mesh,
        in_specs=placed,
        out_specs=(
            P("rows", None, "chan"),
            P("rows", "chan"),
            P("chan", "rows"),
            P(None, None, "chan"),
        ),
        check_vma=False,
    )
```

```python
import math

import jax
import jax.numpy as jnp
from jax import lax
from jax.sharding import PartitionSpec as P


def halo(cells, width):
    count = lax.axis_size("rows")
    ends = count - 1
    head = cells[:width]
    tail = cells[cells.shape[0] - width :]
    above = lax.ppermute(tail, "rows", [(i, i + 1) for i in range(ends)])
    below = lax.ppermute(head, "rows", [(i + 1, i) for i in range(ends)])
    return above, below


def conv_taps(padded, kernel, height, width):
    result = jnp.zeros((height, width, kernel.shape[2]), jnp.float32)
    for tap_row in range(7):
        for tap_col in range(7):
            window = padded[tap_row : tap_row + height, tap_col : tap_col + width].astype(
                jnp.float32
            )
            result = result + window * kernel[tap_row, tap_col]
    return result


def conv_back(grad_pad, kernel, height, width):
    result = jnp.zeros((height, width, kernel.shape[2]), jnp.float32)
    for tap_row in range(7):
        for tap_col in range(7):
            window = grad_pad[
                6 - tap_row : 6 - tap_row + height, 6 - tap_col : 6 - tap_col + width
            ].astype(jnp.float32)
            result = result + window * kernel[tap_row, tap_col]
    return result


def kernel_terms(grad_conv, padded, height, width, tap_rows):
    grad_float = grad_conv.astype(jnp.float32)
    rows_list = []
    for tap_row in tap_rows:
        cols_list = []
        for tap_col in range(7):
            window = padded[tap_row : tap_row + height, tap_col : tap_col + width].astype(
                jnp.float32
            )
            cols_list.append(jnp.sum(grad_float * window, axis=(0, 1)))
        rows_list.append(jnp.stack(cols_list))
    return jnp.stack(rows_list)


def gelu_tanh(value):
    return jax.nn.gelu(value, approximate=True)


def chip_at(place, chips):
    place = lax.rem(place, chips)
    half = chips // 2
    return jnp.where(place < half, 2 * place, 2 * (chips - 1 - place) + 1)


def ring_pairs(chips, step):
    def chip(place):
        place = place % chips
        half = chips // 2
        return 2 * place if place < half else 2 * (chips - 1 - place) + 1

    return [
        (2 * chip(p) + core, 2 * chip(p + step) + core) for p in range(chips) for core in range(2)
    ]


def tie(value, *first):
    return lax.optimization_barrier((value, first))[0]


def ring_piece(part, position, side, chips):
    share = part.shape[0] // chips
    half = share // 2
    return lax.dynamic_slice_in_dim(
        part, chip_at(position, chips) * share + side * half, half, 0
    )


def ring_first(part, place, chips):
    return [ring_piece(part, place + chips - 1, 0, chips), ring_piece(part, place + 1, 1, chips)]


def ring_step(part, sums, step, place, chips):
    result = []
    for side, way in ((0, 1), (1, -1)):
        got = lax.ppermute(sums[side], "rows", ring_pairs(chips, way))
        own = ring_piece(part, place + 2 * chips - way * (2 + step), side, chips)
        total = got.astype(jnp.float32) + own.astype(jnp.float32)
        result.append(total.astype(jnp.bfloat16))
    return result


def own_rows(sums, core, swap):
    mine = jnp.where(core == 0, sums[0], sums[1])
    theirs = jnp.where(core == 0, sums[1], sums[0])
    got = lax.ppermute(theirs, "rows", swap)
    first = jnp.where(core == 0, mine, got)
    second = jnp.where(core == 0, got, mine)
    return jnp.concatenate([first, second], axis=1).astype(jnp.float32)


def shards(feature, kernel, ln_gain, layer_scale, w_in, w_out, cotangent):
    height, width, local_ch = feature.shape
    channels = cotangent.shape[2]
    pixels = height * width
    rows = lax.axis_size("rows")
    chan = lax.axis_size("chan")
    chips = rows // 2
    me = lax.axis_index("rows")
    lane = lax.axis_index("chan")
    core = lax.rem(me, 2)
    chip = lax.div(me, 2)
    level = lax.div(chip, 2)
    place = jnp.where(lax.rem(chip, 2) == 0, level, chips - 1 - level)
    swap = [(i, i ^ 1) for i in range(rows)]
    cross = [(0, 1), (1, 0)]
    scale = 1.0 / math.sqrt(height * rows * width)
    offset = lane * local_ch
    units = w_in.shape[1] // 2

    above, below = halo(feature, 3)
    grad_mixed = (cotangent.reshape(pixels, channels).astype(jnp.float32) * layer_scale).astype(
        jnp.bfloat16
    )
    mixed_both = jnp.concatenate([grad_mixed, lax.ppermute(grad_mixed, "rows", swap)], axis=0)
    in_part = lax.dynamic_slice_in_dim(w_in, core * units, units, 1)
    out_part = lax.dynamic_slice_in_dim(w_out, core * units, units, 0)
    grad_activ = lax.dot_general(
        mixed_both, out_part, (((1,), (1,)), ((), ())), preferred_element_type=jnp.float32
    )
    rimmed = jnp.concatenate([above, feature, below], axis=0)
    padded = jnp.pad(rimmed, ((0, 0), (3, 3), (0, 0)))
    conv_local = conv_taps(padded, kernel, height, width).astype(jnp.bfloat16)
    conv_local = conv_local.reshape(pixels, local_ch)
    if chan == 2:
        conv_other = lax.ppermute(conv_local, "chan", cross)
        conv_other = tie(conv_other, grad_activ)
        conv_full = jnp.concatenate(
            [
                jnp.where(lane == 0, conv_local, conv_other),
                jnp.where(lane == 0, conv_other, conv_local),
            ],
            axis=1,
        )
    else:
        conv_full = lax.all_gather(conv_local, "chan", axis=1, tiled=True)
    values = conv_full.astype(jnp.float32)
    mean = jnp.mean(values, axis=1, keepdims=True)
    centred = values - mean
    var = jnp.mean(centred * centred, axis=1, keepdims=True)
    rstd = 1.0 / jnp.sqrt(var + 1e-06)
    nhat = centred * rstd
    normed = (nhat * ln_gain).astype(jnp.bfloat16)
    normed_both = jnp.concatenate([normed, lax.ppermute(normed, "rows", swap)], axis=0)
    hidden = jnp.dot(normed_both, in_part, preferred_element_type=jnp.float32)
    activ = gelu_tanh(hidden).astype(jnp.bfloat16)
    grad_hidden = jax.vjp(gelu_tanh, hidden)[1](grad_activ)[0].astype(jnp.bfloat16)

    def pixel_sum(left, right):
        total = lax.dot_general(
            left, right, (((0,), (0,)), ((), ())), preferred_element_type=jnp.float32
        )
        return (total * scale).astype(jnp.bfloat16)

    def back(grads):
        return lax.dot_general(
            grads, in_part, (((1,), (1,)), ((), ())), preferred_element_type=jnp.float32
        )

    out_total = pixel_sum(mixed_both, activ)
    back_other = lax.ppermute(back(grad_hidden[pixels:]).astype(jnp.bfloat16), "rows", swap)
    in_total = pixel_sum(normed_both, grad_hidden)
    back_own = back(tie(grad_hidden[:pixels], in_total)) + back_other.astype(jnp.float32)

    scaled_part = back_own * ln_gain
    first_part = jnp.sum(scaled_part, axis=1)
    second_part = jnp.sum(scaled_part * nhat, axis=1)
    pair = jnp.stack([first_part, second_part])
    if chan == 2:
        kept = lax.dynamic_slice_in_dim(back_own, offset, local_ch, 1)
        given = lax.dynamic_slice_in_dim(back_own, local_ch - offset, local_ch, 1)
        sent = (given.astype(jnp.bfloat16), pair)
        got = lax.ppermute(sent[0], "chan", cross).astype(jnp.float32)
        grad_normed = kept + got
        pair = pair + lax.ppermute(pair, "chan", cross)
    else:
        sent = (back_own, pair)
        grad_normed = lax.psum_scatter(
            back_own.astype(jnp.bfloat16), "chan", scatter_dimension=1, tiled=True
        ).astype(jnp.float32)
        pair = lax.psum(pair, "chan")
    first_mean = pair[0][:, None] / channels
    second_mean = pair[1][:, None] / channels
    nhat_own = (conv_local.astype(jnp.float32) - mean) * rstd
    scaled = grad_normed * lax.dynamic_slice_in_dim(ln_gain, offset, local_ch, 0)
    grad_local = rstd * (scaled - first_mean - nhat_own * second_mean)
    grad_conv = grad_local.astype(jnp.bfloat16).reshape(height, width, local_ch)
    grad_above, grad_below = halo(grad_conv, 3)
    grad_rimmed = jnp.concatenate([grad_above, grad_conv, grad_below], axis=0)
    grad_pad = jnp.pad(grad_rimmed, ((0, 0), (3, 3), (0, 0)))
    cot_own = lax.dynamic_slice_in_dim(cotangent, offset, local_ch, 2).astype(jnp.float32)

    def terms(grads, tap_rows):
        return (kernel_terms(grads, padded, height, width, tap_rows) * scale).astype(
            jnp.bfloat16
        )

    kernel_sum = None
    grad_feature = None
    span = 1
    totals = [out_total, in_total]
    sums = [ring_first(total, place, chips) for total in totals]
    last = chips - 2
    for step in range(chips - 1):
        for which in range(2):
            if step == 1 and which == 1:
                sums[which] = tie(sums[which], sent)
            if step == 3 and which == 0:
                sums[which] = tie(sums[which], grad_conv)
            if step == 4 and which == 0:
                kernel_sum = terms(tie(grad_conv, early), range(7))
                sums[which] = tie(sums[which], kernel_sum)
            if step == last and which == 1:
                grad_feature = (
                    cot_own + conv_back(tie(grad_pad, middle), kernel, height, width)
                ).astype(jnp.bfloat16)
                sums[which] = tie(sums[which], grad_feature)
            if step > 4 and span < rows:
                other = lax.ppermute(kernel_sum, "rows", [(i, i ^ span) for i in range(rows)])
                total = kernel_sum.astype(jnp.float32) + other.astype(jnp.float32)
                span *= 2
                kernel_sum = total if span >= rows else total.astype(jnp.bfloat16)
                sums[which] = tie(sums[which], kernel_sum)
            sums[which] = ring_step(totals[which], sums[which], step, place, chips)
        if step == 1:
            early = list(sums)
        if step == 3:
            middle = list(sums)
    while span < rows:
        other = lax.ppermute(kernel_sum, "rows", [(i, i ^ span) for i in range(rows)])
        total = kernel_sum.astype(jnp.float32) + other.astype(jnp.float32)
        span *= 2
        kernel_sum = total if span >= rows else total.astype(jnp.bfloat16)
    grad_w_out = own_rows(sums[0], core, swap).T
    grad_w_in = own_rows(sums[1], core, swap)
    return (grad_feature, grad_w_in, grad_w_out, kernel_sum)


def solution(mesh):
    placed = (
        P("rows", None, "chan"),
        P(None, None, "chan"),
        P(),
        P(),
        P(None, "chan"),
        P("chan", None),
        P("rows", None, None),
    )
    return jax.shard_map(
        shards,
        mesh=mesh,
        in_specs=placed,
        out_specs=(
            P("rows", None, "chan"),
            P("rows", "chan"),
            P("chan", "rows"),
            P(None, None, "chan"),
        ),
        check_vma=False,
    )
```

```python
import math

import jax
import jax.numpy as jnp
from jax import lax
from jax.sharding import PartitionSpec as P


def halo(cells, width):
    count = lax.axis_size("rows")
    ends = count - 1
    head = cells[:width]
    tail = cells[cells.shape[0] - width :]
    above = lax.ppermute(tail, "rows", [(i, i + 1) for i in range(ends)])
    below = lax.ppermute(head, "rows", [(i + 1, i) for i in range(ends)])
    return above, below


def conv_line(cells, kernel, line, rim, height, width, begun):
    own = range(3 - line, 3 - line + height)
    if begun is None:
        result = jnp.zeros((1, width, kernel.shape[2]), jnp.float32)
        tap_rows = [tap for tap in range(7) if tap in own]
    else:
        result = begun
        tap_rows = [tap for tap in range(7) if tap not in own]
    for tap_row in tap_rows:
        row = line + tap_row - 3 + rim
        for tap_col in range(7):
            window = cells[row : row + 1, tap_col : tap_col + width].astype(jnp.float32)
            result = result + window * kernel[tap_row, tap_col]
    return result


def conv_back(grad_pad, kernel, height, width):
    result = jnp.zeros((height, width, kernel.shape[2]), jnp.float32)
    for tap_row in range(7):
        for tap_col in range(7):
            window = grad_pad[
                6 - tap_row : 6 - tap_row + height, 6 - tap_col : 6 - tap_col + width
            ].astype(jnp.float32)
            result = result + window * kernel[tap_row, tap_col]
    return result


def kernel_terms(grad_conv, padded, height, width, tap_rows):
    grad_float = grad_conv.astype(jnp.float32)
    rows_list = []
    for tap_row in tap_rows:
        cols_list = []
        for tap_col in range(7):
            window = padded[tap_row : tap_row + height, tap_col : tap_col + width].astype(
                jnp.float32
            )
            cols_list.append(jnp.sum(grad_float * window, axis=(0, 1)))
        rows_list.append(jnp.stack(cols_list))
    return jnp.stack(rows_list)


def gelu_tanh(value):
    return jax.nn.gelu(value, approximate=True)


def chip_at(place, chips):
    place = lax.rem(place, chips)
    half = chips // 2
    return jnp.where(place < half, 2 * place, 2 * (chips - 1 - place) + 1)


def ring_pairs(chips, step):
    def chip(place):
        place = place % chips
        half = chips // 2
        return 2 * place if place < half else 2 * (chips - 1 - place) + 1

    return [
        (2 * chip(p) + core, 2 * chip(p + step) + core) for p in range(chips) for core in range(2)
    ]


def tie(value, *first):
    return lax.optimization_barrier((value, first))[0]


def ring_piece(part, position, side, chips):
    share = part.shape[0] // chips
    half = share // 2
    return lax.dynamic_slice_in_dim(
        part, chip_at(position, chips) * share + side * half, half, 0
    )


def ring_first(part, place, chips):
    return [ring_piece(part, place + chips - 1, 0, chips), ring_piece(part, place + 1, 1, chips)]


def ring_step(part, sums, step, place, chips):
    result = []
    for side, way in ((0, 1), (1, -1)):
        got = lax.ppermute(sums[side], "rows", ring_pairs(chips, way))
        own = ring_piece(part, place + 2 * chips - way * (2 + step), side, chips)
        total = got.astype(jnp.float32) + own.astype(jnp.float32)
        result.append(total.astype(jnp.bfloat16))
    return result


def own_rows(sums, core, swap):
    mine = jnp.where(core == 0, sums[0], sums[1])
    theirs = jnp.where(core == 0, sums[1], sums[0])
    got = lax.ppermute(theirs, "rows", swap)
    first = jnp.where(core == 0, mine, got)
    second = jnp.where(core == 0, got, mine)
    return jnp.concatenate([first, second], axis=1).astype(jnp.float32)


def shards(feature, kernel, ln_gain, layer_scale, w_in, w_out, cotangent):
    height, width, local_ch = feature.shape
    channels = cotangent.shape[2]
    pixels = height * width
    rows = lax.axis_size("rows")
    chan = lax.axis_size("chan")
    chips = rows // 2
    me = lax.axis_index("rows")
    lane = lax.axis_index("chan")
    core = lax.rem(me, 2)
    chip = lax.div(me, 2)
    level = lax.div(chip, 2)
    place = jnp.where(lax.rem(chip, 2) == 0, level, chips - 1 - level)
    swap = [(i, i ^ 1) for i in range(rows)]
    cross = [(0, 1), (1, 0)]
    scale = 1.0 / math.sqrt(height * rows * width)
    offset = lane * local_ch
    units = w_in.shape[1] // 2

    above, below = halo(feature, 3)
    grad_mixed = (cotangent.reshape(pixels, channels).astype(jnp.float32) * layer_scale).astype(
        jnp.bfloat16
    )
    mixed_both = jnp.concatenate([grad_mixed, lax.ppermute(grad_mixed, "rows", swap)], axis=0)
    in_part = lax.dynamic_slice_in_dim(w_in, core * units, units, 1)
    out_part = lax.dynamic_slice_in_dim(w_out, core * units, units, 0)
    grad_activ = lax.dot_general(
        mixed_both, out_part, (((1,), (1,)), ((), ())), preferred_element_type=jnp.float32
    )
    inner = jnp.pad(feature, ((0, 0), (3, 3), (0, 0)))
    begun = [conv_line(inner, kernel, line, 0, height, width, None) for line in range(height)]
    above, below, begun = lax.optimization_barrier((above, below, begun))
    rimmed = jnp.concatenate([above, feature, below], axis=0)
    padded = jnp.pad(rimmed, ((0, 0), (3, 3), (0, 0)))
    lines = [
        conv_line(padded, kernel, line, 3, height, width, begun[line]) for line in range(height)
    ]
    conv_local = jnp.concatenate(lines, axis=0).astype(jnp.bfloat16)
    conv_local = conv_local.reshape(pixels, local_ch)
    if chan == 2:
        conv_other = lax.ppermute(conv_local, "chan", cross)
        conv_other = tie(conv_other, grad_activ)
        conv_full = jnp.concatenate(
            [
                jnp.where(lane == 0, conv_local, conv_other),
                jnp.where(lane == 0, conv_other, conv_local),
            ],
            axis=1,
        )
    else:
        conv_full = lax.all_gather(conv_local, "chan", axis=1, tiled=True)
    values = conv_full.astype(jnp.float32)
    mean = jnp.mean(values, axis=1, keepdims=True)
    centred = values - mean
    var = jnp.mean(centred * centred, axis=1, keepdims=True)
    rstd = 1.0 / jnp.sqrt(var + 1e-06)
    nhat = centred * rstd
    normed = (nhat * ln_gain).astype(jnp.bfloat16)
    normed_both = jnp.concatenate([normed, lax.ppermute(normed, "rows", swap)], axis=0)
    hidden = jnp.dot(normed_both, in_part, preferred_element_type=jnp.float32)
    activ = gelu_tanh(hidden).astype(jnp.bfloat16)
    grad_hidden = jax.vjp(gelu_tanh, hidden)[1](grad_activ)[0].astype(jnp.bfloat16)

    def pixel_sum(left, right):
        total = lax.dot_general(
            left, right, (((0,), (0,)), ((), ())), preferred_element_type=jnp.float32
        )
        return (total * scale).astype(jnp.bfloat16)

    def back(grads):
        return lax.dot_general(
            grads, in_part, (((1,), (1,)), ((), ())), preferred_element_type=jnp.float32
        )

    out_total = pixel_sum(mixed_both, activ)
    back_other = lax.ppermute(back(grad_hidden[pixels:]).astype(jnp.bfloat16), "rows", swap)
    in_total = pixel_sum(normed_both, grad_hidden)
    back_own = back(tie(grad_hidden[:pixels], in_total)) + back_other.astype(jnp.float32)

    scaled_part = back_own * ln_gain
    first_part = jnp.sum(scaled_part, axis=1)
    second_part = jnp.sum(scaled_part * nhat, axis=1)
    pair = jnp.stack([first_part, second_part])
    if chan == 2:
        kept = lax.dynamic_slice_in_dim(back_own, offset, local_ch, 1)
        given = lax.dynamic_slice_in_dim(back_own, local_ch - offset, local_ch, 1)
        sent = (given.astype(jnp.bfloat16), pair)
        got = lax.ppermute(sent[0], "chan", cross).astype(jnp.float32)
        grad_normed = kept + got
        pair = pair + lax.ppermute(pair, "chan", cross)
    else:
        sent = (back_own, pair)
        grad_normed = lax.psum_scatter(
            back_own.astype(jnp.bfloat16), "chan", scatter_dimension=1, tiled=True
        ).astype(jnp.float32)
        pair = lax.psum(pair, "chan")
    first_mean = pair[0][:, None] / channels
    second_mean = pair[1][:, None] / channels
    nhat_own = (conv_local.astype(jnp.float32) - mean) * rstd
    scaled = grad_normed * lax.dynamic_slice_in_dim(ln_gain, offset, local_ch, 0)
    grad_local = rstd * (scaled - first_mean - nhat_own * second_mean)
    grad_conv = grad_local.astype(jnp.bfloat16).reshape(height, width, local_ch)
    grad_above, grad_below = halo(grad_conv, 3)
    grad_rimmed = jnp.concatenate([grad_above, grad_conv, grad_below], axis=0)
    grad_pad = jnp.pad(grad_rimmed, ((0, 0), (3, 3), (0, 0)))
    cot_own = lax.dynamic_slice_in_dim(cotangent, offset, local_ch, 2).astype(jnp.float32)

    def terms(grads, tap_rows):
        return (kernel_terms(grads, padded, height, width, tap_rows) * scale).astype(
            jnp.bfloat16
        )

    def spread(summed, span):
        width_of = min(4, rows // span)
        total = summed.astype(jnp.float32)
        for other in range(1, width_of):
            pairs = [(i, i ^ (span * other)) for i in range(rows)]
            total = total + lax.ppermute(summed, "rows", pairs).astype(jnp.float32)
        span *= width_of
        return (total if span >= rows else total.astype(jnp.bfloat16)), span

    kernel_sum = None
    grad_feature = None
    span = 1
    totals = [out_total, in_total]
    sums = [ring_first(total, place, chips) for total in totals]
    last = chips - 2
    for step in range(chips - 1):
        for which in range(2):
            if step == 1 and which == 1:
                sums[which] = tie(sums[which], sent)
            if step == 3 and which == 0:
                sums[which] = tie(sums[which], grad_conv)
            if step == 4 and which == 0:
                kernel_sum = terms(tie(grad_conv, early), range(7))
                sums[which] = tie(sums[which], kernel_sum)
            if step == 5 and which == 1:
                kernel_sum, span = spread(kernel_sum, span)
                sums[which] = tie(sums[which], kernel_sum)
            if step == last and which == 1:
                grad_feature = (
                    cot_own + conv_back(tie(grad_pad, middle), kernel, height, width)
                ).astype(jnp.bfloat16)
                sums[which] = tie(sums[which], grad_feature)
            sums[which] = ring_step(totals[which], sums[which], step, place, chips)
        if step == 1:
            early = list(sums)
        if step == 3:
            middle = list(sums)
    while span < rows:
        kernel_sum, span = spread(kernel_sum, span)
    sums[1] = tie(sums[1], kernel_sum)
    grad_w_out = own_rows(sums[0], core, swap).T
    grad_w_in = own_rows(sums[1], core, swap)
    return (grad_feature, grad_w_in, grad_w_out, kernel_sum)


def solution(mesh):
    placed = (
        P("rows", None, "chan"),
        P(None, None, "chan"),
        P(),
        P(),
        P(None, "chan"),
        P("chan", None),
        P("rows", None, None),
    )
    return jax.shard_map(
        shards,
        mesh=mesh,
        in_specs=placed,
        out_specs=(
            P("rows", None, "chan"),
            P("rows", "chan"),
            P("chan", "rows"),
            P(None, None, "chan"),
        ),
        check_vma=False,
    )
```

```python
import math

import jax
import jax.numpy as jnp
from jax import lax
from jax.sharding import PartitionSpec as P


def halo(cells, width):
    count = lax.axis_size("rows")
    ends = count - 1
    head = cells[:width]
    tail = cells[cells.shape[0] - width :]
    above = lax.ppermute(tail, "rows", [(i, i + 1) for i in range(ends)])
    below = lax.ppermute(head, "rows", [(i + 1, i) for i in range(ends)])
    return above, below


def conv_taps(padded, kernel, height, width):
    result = jnp.zeros((height, width, kernel.shape[2]), jnp.float32)
    for tap_row in range(7):
        for tap_col in range(7):
            window = padded[tap_row : tap_row + height, tap_col : tap_col + width].astype(
                jnp.float32
            )
            result = result + window * kernel[tap_row, tap_col]
    return result


def conv_back(grad_pad, kernel, height, width):
    result = jnp.zeros((height, width, kernel.shape[2]), jnp.float32)
    for tap_row in range(7):
        for tap_col in range(7):
            window = grad_pad[
                6 - tap_row : 6 - tap_row + height, 6 - tap_col : 6 - tap_col + width
            ].astype(jnp.float32)
            result = result + window * kernel[tap_row, tap_col]
    return result


def kernel_terms(grad_conv, padded, height, width, tap_rows):
    grad_float = grad_conv.astype(jnp.float32)
    rows_list = []
    for tap_row in tap_rows:
        cols_list = []
        for tap_col in range(7):
            window = padded[tap_row : tap_row + height, tap_col : tap_col + width].astype(
                jnp.float32
            )
            cols_list.append(jnp.sum(grad_float * window, axis=(0, 1)))
        rows_list.append(jnp.stack(cols_list))
    return jnp.stack(rows_list)


def gelu_tanh(value):
    return jax.nn.gelu(value, approximate=True)


def chip_at(place, chips):
    place = lax.rem(place, chips)
    half = chips // 2
    return jnp.where(place < half, 2 * place, 2 * (chips - 1 - place) + 1)


def ring_pairs(chips, step):
    def chip(place):
        place = place % chips
        half = chips // 2
        return 2 * place if place < half else 2 * (chips - 1 - place) + 1

    return [
        (2 * chip(p) + core, 2 * chip(p + step) + core) for p in range(chips) for core in range(2)
    ]


def tie(value, *first):
    return lax.optimization_barrier((value, first))[0]


def ring_piece(part, position, side, chips):
    share = part.shape[0] // chips
    half = share // 2
    return lax.dynamic_slice_in_dim(
        part, chip_at(position, chips) * share + side * half, half, 0
    )


def ring_first(part, place, chips):
    return [ring_piece(part, place + chips - 1, 0, chips), ring_piece(part, place + 1, 1, chips)]


def ring_step(part, sums, step, place, chips):
    result = []
    for side, way in ((0, 1), (1, -1)):
        got = lax.ppermute(sums[side], "rows", ring_pairs(chips, way))
        own = ring_piece(part, place + 2 * chips - way * (2 + step), side, chips)
        total = got.astype(jnp.float32) + own.astype(jnp.float32)
        result.append(total.astype(jnp.bfloat16))
    return result


def own_rows(sums, core, swap):
    mine = jnp.where(core == 0, sums[0], sums[1])
    theirs = jnp.where(core == 0, sums[1], sums[0])
    got = lax.ppermute(theirs, "rows", swap)
    first = jnp.where(core == 0, mine, got)
    second = jnp.where(core == 0, got, mine)
    return jnp.concatenate([first, second], axis=1).astype(jnp.float32)


def shards(feature, kernel, ln_gain, layer_scale, w_in, w_out, cotangent):
    height, width, local_ch = feature.shape
    channels = cotangent.shape[2]
    pixels = height * width
    rows = lax.axis_size("rows")
    chan = lax.axis_size("chan")
    chips = rows // 2
    me = lax.axis_index("rows")
    lane = lax.axis_index("chan")
    core = lax.rem(me, 2)
    chip = lax.div(me, 2)
    level = lax.div(chip, 2)
    place = jnp.where(lax.rem(chip, 2) == 0, level, chips - 1 - level)
    swap = [(i, i ^ 1) for i in range(rows)]
    cross = [(0, 1), (1, 0)]
    scale = 1.0 / math.sqrt(height * rows * width)
    offset = lane * local_ch
    units = w_in.shape[1] // 2

    above, below = halo(feature, 3)
    grad_mixed = (cotangent.reshape(pixels, channels).astype(jnp.float32) * layer_scale).astype(
        jnp.bfloat16
    )
    mixed_both = jnp.concatenate([grad_mixed, lax.ppermute(grad_mixed, "rows", swap)], axis=0)
    in_part = lax.dynamic_slice_in_dim(w_in, core * units, units, 1)
    out_part = lax.dynamic_slice_in_dim(w_out, core * units, units, 0)
    grad_activ = lax.dot_general(
        mixed_both, out_part, (((1,), (1,)), ((), ())), preferred_element_type=jnp.float32
    )
    rimmed = jnp.concatenate([above, feature, below], axis=0)
    padded = jnp.pad(rimmed, ((0, 0), (3, 3), (0, 0)))
    conv_local = conv_taps(padded, kernel, height, width).astype(jnp.bfloat16)
    conv_local = conv_local.reshape(pixels, local_ch)
    if chan == 2:
        conv_other = lax.ppermute(conv_local, "chan", cross)
        conv_other = tie(conv_other, grad_activ)
        conv_full = jnp.concatenate(
            [
                jnp.where(lane == 0, conv_local, conv_other),
                jnp.where(lane == 0, conv_other, conv_local),
            ],
            axis=1,
        )
    else:
        conv_full = lax.all_gather(conv_local, "chan", axis=1, tiled=True)
    values = conv_full.astype(jnp.float32)
    mean = jnp.mean(values, axis=1, keepdims=True)
    centred = values - mean
    var = jnp.mean(centred * centred, axis=1, keepdims=True)
    rstd = 1.0 / jnp.sqrt(var + 1e-06)
    nhat = centred * rstd
    normed = (nhat * ln_gain).astype(jnp.bfloat16)
    normed_both = jnp.concatenate([normed, lax.ppermute(normed, "rows", swap)], axis=0)
    hidden = jnp.dot(normed_both, in_part, preferred_element_type=jnp.float32)
    activ = gelu_tanh(hidden).astype(jnp.bfloat16)
    grad_hidden = jax.vjp(gelu_tanh, hidden)[1](grad_activ)[0].astype(jnp.bfloat16)

    def pixel_sum(left, right):
        total = lax.dot_general(
            left, right, (((0,), (0,)), ((), ())), preferred_element_type=jnp.float32
        )
        return (total * scale).astype(jnp.bfloat16)

    def back(grads):
        return lax.dot_general(
            grads, in_part, (((1,), (1,)), ((), ())), preferred_element_type=jnp.float32
        )

    out_total = pixel_sum(mixed_both, activ)
    back_other = lax.ppermute(back(grad_hidden[pixels:]).astype(jnp.bfloat16), "rows", swap)
    in_total = pixel_sum(normed_both, grad_hidden)
    back_own = back(tie(grad_hidden[:pixels], in_total)) + back_other.astype(jnp.float32)

    scaled_part = back_own * ln_gain
    first_part = jnp.sum(scaled_part, axis=1)
    second_part = jnp.sum(scaled_part * nhat, axis=1)
    pair = jnp.stack([first_part, second_part])
    if chan == 2:
        kept = lax.dynamic_slice_in_dim(back_own, offset, local_ch, 1)
        given = lax.dynamic_slice_in_dim(back_own, local_ch - offset, local_ch, 1)
        sent = (given.astype(jnp.bfloat16), pair)
        got = lax.ppermute(sent[0], "chan", cross).astype(jnp.float32)
        grad_normed = kept + got
        pair = pair + lax.ppermute(pair, "chan", cross)
    else:
        sent = (back_own, pair)
        grad_normed = lax.psum_scatter(
            back_own.astype(jnp.bfloat16), "chan", scatter_dimension=1, tiled=True
        ).astype(jnp.float32)
        pair = lax.psum(pair, "chan")
    first_mean = pair[0][:, None] / channels
    second_mean = pair[1][:, None] / channels
    nhat_own = (conv_local.astype(jnp.float32) - mean) * rstd
    scaled = grad_normed * lax.dynamic_slice_in_dim(ln_gain, offset, local_ch, 0)
    grad_local = rstd * (scaled - first_mean - nhat_own * second_mean)
    grad_conv = grad_local.astype(jnp.bfloat16).reshape(height, width, local_ch)
    grad_above, grad_below = halo(grad_conv, 3)
    grad_rimmed = jnp.concatenate([grad_above, grad_conv, grad_below], axis=0)
    grad_pad = jnp.pad(grad_rimmed, ((0, 0), (3, 3), (0, 0)))
    cot_own = lax.dynamic_slice_in_dim(cotangent, offset, local_ch, 2).astype(jnp.float32)

    def terms(grads, tap_rows):
        return (kernel_terms(grads, padded, height, width, tap_rows) * scale).astype(
            jnp.bfloat16
        )

    kernel_sum = None
    grad_feature = None
    span = 1
    totals = [out_total, in_total]
    sums = [ring_first(total, place, chips) for total in totals]
    last = chips - 2
    for step in range(chips - 1):
        for which in range(2):
            if step == 1 and which == 1:
                sums[which] = tie(sums[which], sent)
            if step == 3 and which == 0:
                sums[which] = tie(sums[which], grad_conv)
            if step == 3 and which == 1:
                kernel_sum = terms(tie(grad_conv, early), range(7))
                sums[which] = tie(sums[which], kernel_sum)
            if step == last and which == 1:
                grad_feature = (
                    cot_own + conv_back(tie(grad_pad, middle), kernel, height, width)
                ).astype(jnp.bfloat16)
                sums[which] = tie(sums[which], grad_feature)
            if step > 3 and which == 1 and span < rows:
                other = lax.ppermute(kernel_sum, "rows", [(i, i ^ span) for i in range(rows)])
                total = kernel_sum.astype(jnp.float32) + other.astype(jnp.float32)
                span *= 2
                kernel_sum = total if span >= rows else total.astype(jnp.bfloat16)
                sums[which] = tie(sums[which], kernel_sum)
            sums[which] = ring_step(totals[which], sums[which], step, place, chips)
        if step == 1:
            early = list(sums)
        if step == 3:
            middle = list(sums)
    while span < rows:
        other = lax.ppermute(kernel_sum, "rows", [(i, i ^ span) for i in range(rows)])
        total = kernel_sum.astype(jnp.float32) + other.astype(jnp.float32)
        span *= 2
        kernel_sum = total if span >= rows else total.astype(jnp.bfloat16)
    grad_w_out = own_rows(sums[0], core, swap).T
    grad_w_in = own_rows(sums[1], core, swap)
    return (grad_feature, grad_w_in, grad_w_out, kernel_sum)


def solution(mesh):
    placed = (
        P("rows", None, "chan"),
        P(None, None, "chan"),
        P(),
        P(),
        P(None, "chan"),
        P("chan", None),
        P("rows", None, None),
    )
    return jax.shard_map(
        shards,
        mesh=mesh,
        in_specs=placed,
        out_specs=(
            P("rows", None, "chan"),
            P("rows", "chan"),
            P("chan", "rows"),
            P(None, None, "chan"),
        ),
        check_vma=False,
    )
```
